512 devices in a mesh: chan: 64 (over x, y, z_hi, core), seg: 8 (over z_lo).
Axes of the slice: x: 4, y: 4, z: 16 (z_hi: 2, z_lo: 8; z = z_hi * 8 + z_lo), core: 2. Of those that a mesh axis runs over, the one named last changes fastest.
Arguments:
- records: bfloat16 [8, 16384, 4, 512], P('seg', 'chan'), may hold values from -6 to 6
- alive: int32 [16384], P('chan'), may hold values 0 or 1
- offsets: int32 [64, 16], P('chan'), may hold values from 1 to 256, as said below
Outputs:
- correlations: bfloat16 [16, 16384, 256], P('seg', 'chan')
The draws below stay inside these ranges and needn't reach their ends.
Inputs may be any that keep to these rules, and one draw needn't show every extreme that they name: Each block's 16 offsets are distinct and one of them is 256.
All inputs are finite; a program needn't handle non-finite values. No bound on the sum of `alive` on one device may be relied on, other than what follows from the above.
Results may differ from the reference program's by a relative error of at most 0.02.
Values may be sent and summed in bfloat16 or wider, within the bound.
A program may use at most 64 MiB of HBM per device.

```python
import jax
import jax.numpy as jnp
from jax import lax

C_DEV = 256
W = 4
WIN = 512
NF = 128
F0 = 1
NL = 256
K = 16
REACH = 256
CHANNELS = 16384
CHAN_BLOCKS = 64
SEGMENTS = 8


def draw_offsets(key, part):
    key = jax.random.fold_in(key, 7)
    block_keys = jax.random.split(key, CHAN_BLOCKS)

    def one_block(block_key):
        first_key, second_key = jax.random.split(block_key)
        picks = jax.random.permutation(first_key, REACH - 1)[:K - 1] + 1
        full = jnp.concatenate([picks.astype(jnp.int32), jnp.full((1,), REACH, jnp.int32)])
        return full[jax.random.permutation(second_key, K)]
    return jax.vmap(one_block)(block_keys).astype(jnp.int32)


def with_ends(values, own_key, least, high):
    longest = values.shape.index(max(values.shape))
    spots = []
    for shift in (0, 1):
        where = [jax.random.randint(jax.random.fold_in(own_key, axis), (), 0, length) for axis, length in enumerate(values.shape)]
        where[longest] = (where[longest] + shift) % values.shape[longest]
        spots.append(tuple(where))
    return values.at[spots[0]].set(least).at[spots[1]].set(high)


def steps_of(stream_key, shape, shards, smallest, largest):
    def one(axis_at, blocks):
        steps = jax.random.uniform(jax.random.fold_in(jax.random.fold_in(stream_key, 6), axis_at), (blocks,), jnp.float32, smallest / len(shards), largest / len(shards))
        return jnp.repeat(jnp.exp(steps), shape[axis_at] // blocks).reshape((-1,) + (1,) * (len(shape) - axis_at - 1))

    gain = one(*shards[0])
    for cut in shards[1:]:
        gain = gain * one(*cut)
    return gain


def centred(stream_key, extent, width, limit, shards=(), kind=jnp.bfloat16):
    loudness = steps_of(stream_key, extent, shards, -0.22, 0.18) if shards else 1.0
    entries = jax.random.normal(stream_key, extent, jnp.float32) * width * loudness
    return jnp.minimum(jnp.maximum(entries, -limit), limit).astype(kind)


def setup_inputs(seed: int = 0) -> dict:
    splits = jax.random.split(jax.random.key(seed), 4)
    records = centred(splits[0], (SEGMENTS, CHANNELS, W, WIN), 1.0, 6.0, ((0, 8), (1, 64)))
    alive = with_ends((jax.random.randint(splits[1], (CHANNELS,), 0, 8) < 7).astype(jnp.int32), jax.random.fold_in(splits[1], 1), 0, 1)
    offsets = draw_offsets(jax.random.fold_in(splits[3], 71), 0)
    return dict(records=records, alive=alive, offsets=offsets)


eps = 1e-06

def forward_table():
    times = jnp.arange(WIN, dtype=jnp.int32)[:, None]
    bins = F0 + jnp.arange(NF, dtype=jnp.int32)[None, :]
    angle = (times * bins % WIN).astype(jnp.float32) * (2.0 * jnp.pi / WIN)
    return jnp.concatenate([jnp.cos(angle), -jnp.sin(angle)], axis=1).astype(jnp.bfloat16)

def lag_table():
    bins = F0 + jnp.arange(NF, dtype=jnp.int32)[:, None]
    lags = jnp.arange(NL, dtype=jnp.int32)[None, :] - NL // 2
    angle = (bins * lags % WIN).astype(jnp.float32) * (2.0 * jnp.pi / WIN)
    return jnp.concatenate([jnp.cos(angle), -jnp.sin(angle)], axis=0) / NF

def whiten(raw, live, table):
    count = raw.shape[0]
    spectra = jnp.dot(raw.reshape(count * W, WIN), table, preferred_element_type=jnp.float32)
    spectra = spectra.reshape(count, W, 2 * NF)
    power = lax.optimization_barrier(jnp.mean(spectra * spectra, axis=-1, keepdims=True))
    scaled = spectra * lax.rsqrt(power + eps) * live.astype(jnp.float32)[:, None, None]
    return scaled.astype(jnp.bfloat16)

def pair_product(first, second):
    first = first.astype(jnp.float32)
    second = second.astype(jnp.float32)
    first_re, first_im = (first[..., :NF], first[..., NF:])
    second_re, second_im = (second[..., :NF], second[..., NF:])
    real_part = lax.optimization_barrier(jnp.sum(first_re * second_re + first_im * second_im, axis=1))
    imag_part = lax.optimization_barrier(jnp.sum(first_im * second_re - first_re * second_im, axis=1))
    return jnp.concatenate([real_part, imag_part], axis=-1)

def reference(records, alive, offsets):
    table = forward_table()
    blocks = jnp.arange(CHANNELS, dtype=jnp.int32) // C_DEV
    total = jnp.zeros((K, CHANNELS, 2 * NF), jnp.float32)
    for segment in range(SEGMENTS):
        white = whiten(records[segment], alive, table)
        padded = jnp.concatenate([white, jnp.zeros((C_DEV, W, 2 * NF), jnp.bfloat16)], axis=0)

        def one_slot(slot):
            index = jnp.arange(CHANNELS, dtype=jnp.int32) + offsets[blocks, slot].astype(jnp.int32)
            return pair_product(white, padded[index])
        pairs = lax.map(one_slot, jnp.arange(K, dtype=jnp.int32))
        total = total + lax.optimization_barrier(pairs.astype(jnp.bfloat16)).astype(jnp.float32)
    result = jnp.einsum('kcf,fl->kcl', total, lag_table(), precision=lax.Precision.HIGHEST)
    return result.astype(jnp.bfloat16)
```

```python
import functools

import jax
import jax.numpy as jnp
import numpy as np
from jax import lax
from jax.experimental import pallas as pl
from jax.experimental.pallas import tpu as pltpu
from jax.sharding import PartitionSpec as P

W = 4
WIN = 512
NF = 128
F0 = 1
NL = 256
K = 16
C = 256
SEGS = 8
CHIPS = 16
BINS = NF // CHIPS
PHASES = 2
LANES = 128
eps = 1e-06
MESH = pl.DeviceIdType.MESH


def bin_order():
    chip, part, which = np.meshgrid(np.arange(CHIPS), np.arange(2), np.arange(BINS), indexing="ij")
    return (F0 + chip * BINS + which).reshape(-1), part.reshape(-1)


def forward_table():
    bins, part = bin_order()
    turn = (bins[:, None] * np.arange(WIN)[None, :]) % WIN
    angle = turn * (2.0 * np.pi / WIN)
    rows = np.where(part[:, None] == 0, np.cos(angle), -np.sin(angle))
    return jnp.asarray(rows.astype(np.float32)).astype(jnp.bfloat16)


def lag_table():
    bins, part = bin_order()
    turn = (bins[:, None] * (np.arange(NL)[None, :] - NL // 2)) % WIN
    angle = turn * (2.0 * np.pi / WIN)
    rows = np.where(part[:, None] == 0, np.cos(angle), -np.sin(angle)) / NF
    return jnp.asarray(rows.astype(np.float32))


def kernel(columns, rec_ref, alive_ref, off_ref, tab_ref, lag_ref, out_ref,
           send, recv, rim, wide, totals, res_send, res_recv, off_src, off_recv, off_smem,
           send_sem, recv_sem, rim_send_sem, rim_recv_sem, res_send_sem, res_recv_sem,
           off_send_sem, off_recv_sem, off_local_sem):
    chan = lax.axis_index("chan")
    seg = lax.axis_index("seg")
    core = chan % 2
    zh = (chan // 2) % 2
    col = chan // 4
    z = zh * SEGS + seg
    chain = col * 2 + core
    chains = columns * 2
    before = (chain + chains - 1) % chains
    after = (chain + 1) % chains

    def on_line(chip, which):
        return ((col * 2 + chip // SEGS) * 2 + which, chip % SEGS)

    def on_chain(link):
        return (((link // 2) * 2 + zh) * 2 + link % 2, seg)

    barrier = pltpu.get_barrier_semaphore()

    def greet(t, _):
        chip = (z + t) % CHIPS

        @pl.when(jnp.logical_or(chip != z, zh != core))
        def _():
            pl.semaphore_signal(barrier, 1, device_id=on_line(chip, zh), device_id_type=MESH)
        which = t % 2
        other = core * SEGS + t // 2

        @pl.when(jnp.logical_or(other != z, which != core))
        def _():
            pl.semaphore_signal(barrier, 1, device_id=on_line(other, which), device_id_type=MESH)
        return 0

    lax.fori_loop(0, 2 * SEGS, greet, 0)
    for link in (before, after):
        pl.semaphore_signal(barrier, 1, device_id=on_chain(link), device_id_type=MESH)

    off_src[...] = jnp.zeros_like(off_src)
    off_src[0:1, 0:K] = off_ref[...]
    live = alive_ref[...].astype(jnp.float32)

    def white_copy(phase, chip):
        return pltpu.make_async_remote_copy(
            src_ref=send.at[phase, chip], dst_ref=recv.at[phase, pl.ds(core * 2, 2), seg],
            send_sem=send_sem.at[phase, chip], recv_sem=recv_sem.at[phase, core, seg],
            device_id=on_line(chip, zh), device_id_type=MESH)

    def white_local(phase):
        return pltpu.make_async_copy(
            send.at[phase, z], recv.at[phase, pl.ds(core * 2, 2), seg], recv_sem.at[phase, core, seg])

    def white_wait(phase, block, s):
        pltpu.make_async_copy(
            send.at[phase, 0], recv.at[phase, pl.ds(block * 2, 2), s], recv_sem.at[phase, block, s]).wait()

    def rim_copy(phase, s):
        return pltpu.make_async_remote_copy(
            src_ref=recv.at[phase, pl.ds(0, 2), s], dst_ref=rim.at[phase, :, s],
            send_sem=rim_send_sem.at[phase, s], recv_sem=rim_recv_sem.at[phase, s],
            device_id=on_chain(before), device_id_type=MESH)

    def off_copy(half):
        return pltpu.make_async_remote_copy(
            src_ref=off_src, dst_ref=off_recv.at[core],
            send_sem=off_send_sem.at[half], recv_sem=off_recv_sem.at[core],
            device_id=on_line(half * SEGS + seg, zh), device_id_type=MESH)

    def off_is_remote(half):
        return jnp.logical_or(half != zh, zh != core)

    for phase in range(PHASES):
        spectra = []
        for w in (2 * phase, 2 * phase + 1):
            raw = lax.dot_general(tab_ref[...], rec_ref[w], (((1,), (1,)), ((), ())),
                                  preferred_element_type=jnp.float32)
            power = jnp.sum(raw * raw, axis=0, keepdims=True) * (1.0 / (2 * NF))
            scaled = raw * (lax.rsqrt(power + eps) * live)
            spectra.append(scaled.reshape(CHIPS, 2, 1, BINS, C))
        white = jnp.concatenate(spectra, axis=2).reshape(CHIPS, 4 * BINS, C).astype(jnp.bfloat16)
        for tile in range(2):
            send[phase, :, tile] = white[:, :, tile * LANES:(tile + 1) * LANES]
        if phase == 0:
            met = 4 * SEGS + 2 - 2 * (zh == core).astype(jnp.int32)
            pl.semaphore_wait(barrier, met)
            for half in range(2):
                @pl.when(off_is_remote(half))
                def _():
                    off_copy(half).start()

                @pl.when(jnp.logical_not(off_is_remote(half)))
                def _():
                    pltpu.make_async_copy(off_src, off_recv.at[core], off_recv_sem.at[core]).start()

        def send_white(t, _):
            turn = CHIPS - 1 - t
            away = jnp.where(turn % 2 == 1, (turn + 1) // 2, CHIPS - turn // 2)
            chip = (z + away) % CHIPS

            @pl.when(jnp.logical_or(chip != z, zh != core))
            def _():
                white_copy(phase, chip).start()

            @pl.when(jnp.logical_and(chip == z, zh == core))
            def _():
                white_local(phase).start()
            return 0

        lax.fori_loop(0, CHIPS, send_white, 0)

    for block in range(2):
        pltpu.make_async_copy(off_src, off_recv.at[block], off_recv_sem.at[block]).wait()
        move = pltpu.make_async_copy(off_recv.at[block], off_smem.at[block], off_local_sem.at[block])
        move.start()
        move.wait()

    lane = lax.broadcasted_iota(jnp.int32, (2 * BINS, LANES), 1)
    inside = (chain != chains - 1).astype(jnp.float32)

    def res_copy(block, g):
        return pltpu.make_async_remote_copy(
            src_ref=res_send.at[block, g], dst_ref=res_recv.at[z],
            send_sem=res_send_sem.at[block, g], recv_sem=res_recv_sem.at[z],
            device_id=on_line(core * SEGS + g, block), device_id_type=MESH)

    def res_is_remote(block, g):
        return jnp.logical_or(core * SEGS + g != z, block != core)

    for phase in range(PHASES):
        def forward(s, _):
            white_wait(phase, 0, s)
            rim_copy(phase, s).start()
            for tile in range(2):
                wide[tile, s] = recv[phase, tile, s].astype(jnp.float32)
            return 0

        lax.fori_loop(0, SEGS, forward, 0)

        def take(s, _):
            white_wait(phase, 1, s)
            for tile in range(2, 4):
                wide[tile, s] = recv[phase, tile, s].astype(jnp.float32)
            return 0

        lax.fori_loop(0, SEGS, take, 0)

        def take_rim(s, _):
            rim_copy(phase, s).wait_recv()
            for tile in range(2):
                wide[4 + tile, s] = rim[phase, tile, s].astype(jnp.float32) * inside
            return 0

        lax.fori_loop(0, SEGS, take_rim, 0)

        for block in range(2):
            def slots(g, _):
                for j in range(2):
                    off = jnp.clip(off_smem[block, 0, 2 * g + j], 1, C)
                    skip = (off - 1) // LANES
                    rest = off - skip * LANES
                    first = lane < LANES - rest

                    def one_segment(s, acc):
                        tiles = [pltpu.roll(wide[2 * block + skip + i, s], LANES - rest, 1) for i in range(3)]
                        out = []
                        for tile in range(2):
                            own = wide[2 * block + tile, s]
                            own_re, own_im = own[:2 * BINS], own[2 * BINS:]
                            far_re = jnp.where(first, tiles[tile][:2 * BINS], tiles[tile + 1][:2 * BINS])
                            far_im = jnp.where(first, tiles[tile][2 * BINS:], tiles[tile + 1][2 * BINS:])
                            out.append(acc[2 * tile] + (own_re * far_re + own_im * far_im))
                            out.append(acc[2 * tile + 1] + (own_im * far_re - own_re * far_im))
                        return tuple(out)

                    zero = jnp.zeros((2 * BINS, LANES), jnp.float32)
                    acc = lax.fori_loop(0, SEGS, one_segment, (zero,) * 4, unroll=True)
                    for tile in range(2):
                        parts = [a[:BINS] + a[BINS:] for a in acc[2 * tile:2 * tile + 2]]
                        both = jnp.concatenate(parts, axis=0)
                        if phase > 0:
                            both = both + totals[block, 2 * g + j, tile]
                        if phase < PHASES - 1:
                            totals[block, 2 * g + j, tile] = both
                        else:
                            res_send[block, g, j * 2 * BINS:(j + 1) * 2 * BINS,
                                     tile * LANES:(tile + 1) * LANES] = both.astype(jnp.bfloat16)
                if phase == PHASES - 1:
                    @pl.when(res_is_remote(block, g))
                    def _():
                        res_copy(block, g).start()

                    @pl.when(jnp.logical_not(res_is_remote(block, g)))
                    def _():
                        pltpu.make_async_copy(res_send.at[block, g], res_recv.at[z], res_recv_sem.at[z]).start()
                return 0

            lax.fori_loop(0, SEGS, slots, 0)

    def finish(chip, _):
        pltpu.make_async_copy(res_send.at[0, 0], res_recv.at[chip], res_recv_sem.at[chip]).wait()
        return 0

    lax.fori_loop(0, CHIPS, finish, 0)
    for j in range(2):
        sums = res_recv[:, j * 2 * BINS:(j + 1) * 2 * BINS, :].reshape(2 * NF, C)
        out_ref[j] = lax.dot_general(sums, lag_ref[...], (((0,), (0,)), ((), ())),
                                     preferred_element_type=jnp.float32).astype(jnp.bfloat16)

    def drain(t, _):
        for phase in range(PHASES):
            @pl.when(jnp.logical_or(t != z, zh != core))
            def _():
                white_copy(phase, t).wait_send()
        return 0

    lax.fori_loop(0, CHIPS, drain, 0)

    def drain_more(s, _):
        for phase in range(PHASES):
            rim_copy(phase, s).wait_send()
        for block in range(2):
            @pl.when(res_is_remote(block, s))
            def _():
                res_copy(block, s).wait_send()
        return 0

    lax.fori_loop(0, SEGS, drain_more, 0)
    for half in range(2):
        @pl.when(off_is_remote(half))
        def _():
            off_copy(half).wait_send()


def shards(columns, records, alive, offsets):
    vmem = pl.BlockSpec(memory_space=pltpu.VMEM)
    rec = jnp.transpose(records[0], (1, 0, 2))
    call = pl.pallas_call(
        functools.partial(kernel, columns),
        out_shape=jax.ShapeDtypeStruct((2, C, NL), jnp.bfloat16),
        in_specs=[vmem] * 5,
        out_specs=vmem,
        scratch_shapes=[
            pltpu.VMEM((PHASES, CHIPS, 2, 4 * BINS, LANES), jnp.bfloat16),
            pltpu.VMEM((PHASES, 4, SEGS, 4 * BINS, LANES), jnp.bfloat16),
            pltpu.VMEM((PHASES, 2, SEGS, 4 * BINS, LANES), jnp.bfloat16),
            pltpu.VMEM((6, SEGS, 4 * BINS, LANES), jnp.float32),
            pltpu.VMEM((2, K, 2, 2 * BINS, LANES), jnp.float32),
            pltpu.VMEM((2, SEGS, 4 * BINS, C), jnp.bfloat16),
            pltpu.VMEM((CHIPS, 4 * BINS, C), jnp.bfloat16),
            pltpu.VMEM((8, LANES), jnp.int32),
            pltpu.VMEM((2, 8, LANES), jnp.int32),
            pltpu.SMEM((2, 8, LANES), jnp.int32),
            pltpu.SemaphoreType.DMA((PHASES, CHIPS)),
            pltpu.SemaphoreType.DMA((PHASES, 2, SEGS)),
            pltpu.SemaphoreType.DMA((PHASES, SEGS)),
            pltpu.SemaphoreType.DMA((PHASES, SEGS)),
            pltpu.SemaphoreType.DMA((2, SEGS)),
            pltpu.SemaphoreType.DMA((CHIPS,)),
            pltpu.SemaphoreType.DMA((2,)),
            pltpu.SemaphoreType.DMA((2,)),
            pltpu.SemaphoreType.DMA((2,)),
        ],
        compiler_params=pltpu.CompilerParams(
            collective_id=0, has_side_effects=True, vmem_limit_bytes=32 * 1024 * 1024),
        cost_estimate=pl.CostEstimate(flops=400_000_000, bytes_accessed=3_000_000, transcendentals=1024),
        name="line_correlate",
    )
    return call(rec, alive.reshape(1, C), offsets, forward_table(), lag_table().astype(jnp.bfloat16))


def solution(mesh):
    in_specs = (P("seg", "chan", None, None), P("chan"), P("chan", None))
    out_specs = P("seg", "chan", None)
    body = functools.partial(shards, mesh.shape["chan"] // 4)
    return jax.shard_map(body, mesh=mesh, in_specs=in_specs, out_specs=out_specs, check_vma=False)
```

```python
import functools

import jax
import jax.numpy as jnp
import numpy as np
from jax import lax
from jax.experimental import pallas as pl
from jax.experimental.pallas import tpu as pltpu
from jax.sharding import PartitionSpec as P

W = 4
WIN = 512
NF = 128
F0 = 1
NL = 256
K = 16
C = 256
SEGS = 8
CHIPS = 16
PHASES = 2
BINS = NF // CHIPS // PHASES
ROWS = W * BINS
LANES = 128
GROUP = 8
STEP = 32
eps = 1e-06
MESH = pl.DeviceIdType.MESH
BOTH_MINOR = (((1,), (1,)), ((), ()))


def bin_order():
    phase, chip, part, which = np.meshgrid(
        np.arange(PHASES), np.arange(CHIPS), np.arange(2), np.arange(BINS), indexing="ij")
    return (F0 + (chip * PHASES + phase) * BINS + which).reshape(-1), part.reshape(-1)


def forward_table():
    bins, part = bin_order()
    turn = (bins[:, None] * np.arange(WIN)[None, :]) % WIN
    angle = turn * (2.0 * np.pi / WIN)
    rows = np.where(part[:, None] == 0, np.cos(angle), -np.sin(angle))
    return jnp.asarray(rows.astype(np.float32)).astype(jnp.bfloat16)


def lag_table():
    bins, part = bin_order()
    turn = (bins[:, None] * (np.arange(NL)[None, :] - NL // 2)) % WIN
    angle = turn * (2.0 * np.pi / WIN)
    rows = np.where(part[:, None] == 0, np.cos(angle), -np.sin(angle)) / NF
    return jnp.asarray(rows.astype(np.float32)).astype(jnp.bfloat16)


def identity():
    row = lax.broadcasted_iota(jnp.int32, (C, C), 0)
    column = lax.broadcasted_iota(jnp.int32, (C, C), 1)
    return (row == column).astype(jnp.float32).astype(jnp.bfloat16)


def selector():
    row = lax.broadcasted_iota(jnp.int32, (2 * BINS, 2 * LANES), 0)
    lane = lax.broadcasted_iota(jnp.int32, (2 * BINS, 2 * LANES), 1)
    same = jnp.logical_and(row % BINS == lane % BINS, row // BINS == lane // LANES)
    return same.astype(jnp.float32).astype(jnp.bfloat16)


def kernel(columns, rec_ref, alive_ref, off_ref, tab_ref, lag_ref, out_ref,
           raw, send, recv, rim, far, own, prod, res_send, res_recv, off_src, off_recv, off_smem,
           send_sem, recv_sem, rim_send_sem, rim_recv_sem, res_send_sem, res_recv_sem,
           off_send_sem, off_recv_sem, off_local_sem):
    chan = lax.axis_index("chan")
    seg = lax.axis_index("seg")
    core = chan % 2
    zh = (chan // 2) % 2
    col = chan // 4
    z = zh * SEGS + seg
    chain = col * 2 + core
    chains = columns * 2
    before = (chain + chains - 1) % chains
    after = (chain + 1) % chains

    def on_line(chip, which):
        return ((col * 2 + chip // SEGS) * 2 + which, chip % SEGS)

    def on_chain(link):
        return (((link // 2) * 2 + zh) * 2 + link % 2, seg)

    barrier = pltpu.get_barrier_semaphore()

    def greet(t, _):
        chip = (z + t) % CHIPS

        @pl.when(jnp.logical_or(chip != z, zh != core))
        def _():
            pl.semaphore_signal(barrier, 1, device_id=on_line(chip, zh), device_id_type=MESH)
        which = t % 2
        other = core * SEGS + t // 2

        @pl.when(jnp.logical_or(other != z, which != core))
        def _():
            pl.semaphore_signal(barrier, 1, device_id=on_line(other, which), device_id_type=MESH)
        return 0

    lax.fori_loop(0, 2 * SEGS, greet, 0)
    for link in (before, after):
        pl.semaphore_signal(barrier, 1, device_id=on_chain(link), device_id_type=MESH)

    off_src[...] = jnp.zeros_like(off_src)
    off_src[0:1, 0:K] = off_ref[...]
    live = alive_ref[...].astype(jnp.float32)

    def white_copy(phase, chip):
        return pltpu.make_async_remote_copy(
            src_ref=send.at[phase, chip], dst_ref=recv.at[phase, core, :, seg],
            send_sem=send_sem.at[phase, chip], recv_sem=recv_sem.at[phase, core, seg],
            device_id=on_line(chip, zh), device_id_type=MESH)

    def white_local(phase):
        return pltpu.make_async_copy(
            send.at[phase, z], recv.at[phase, core, :, seg], recv_sem.at[phase, core, seg])

    def white_wait(phase, block, s):
        pltpu.make_async_copy(
            send.at[phase, 0], recv.at[phase, block, :, s], recv_sem.at[phase, block, s]).wait()

    def rim_copy(phase, s):
        return pltpu.make_async_remote_copy(
            src_ref=recv.at[phase, 0, :, s], dst_ref=rim.at[phase, :, s],
            send_sem=rim_send_sem.at[phase, s], recv_sem=rim_recv_sem.at[phase, s],
            device_id=on_chain(before), device_id_type=MESH)

    def off_copy(half):
        return pltpu.make_async_remote_copy(
            src_ref=off_src, dst_ref=off_recv.at[core],
            send_sem=off_send_sem.at[half], recv_sem=off_recv_sem.at[core],
            device_id=on_line(half * SEGS + seg, zh), device_id_type=MESH)

    def off_is_remote(half):
        return jnp.logical_or(half != zh, zh != core)

    scales = []
    for w in range(W):
        spectra = lax.dot_general(tab_ref[...], rec_ref[w], BOTH_MINOR, preferred_element_type=jnp.float32)
        power = jnp.sum(spectra * spectra, axis=0, keepdims=True) * (1.0 / (2 * NF))
        scales.append((lax.rsqrt(power + eps) * live).reshape(1, 1, C))
        raw[w] = spectra.reshape(PHASES * CHIPS, 2 * BINS, C)
    upper = lax.broadcasted_iota(jnp.int32, (1, 2 * BINS, C), 1) < BINS
    some = 4
    for phase in range(PHASES):
        for first in range(0, CHIPS, some):
            real, imag = [], []
            for w in range(0, W, 2):
                at = slice(phase * CHIPS + first, phase * CHIPS + first + some)
                one, two = raw[w, at] * scales[w], raw[w + 1, at] * scales[w + 1]
                real.append(jnp.where(upper, one, pltpu.roll(two, BINS, 1)))
                imag.append(jnp.where(upper, pltpu.roll(one, BINS, 1), two))
            for part, rows in enumerate((real, imag)):
                send[phase, first:first + some, part] = jnp.concatenate(rows, axis=1).astype(jnp.bfloat16)

    met = 4 * SEGS + 2 - 2 * (zh == core).astype(jnp.int32)
    pl.semaphore_wait(barrier, met)
    for half in range(2):
        @pl.when(off_is_remote(half))
        def _():
            off_copy(half).start()

        @pl.when(jnp.logical_not(off_is_remote(half)))
        def _():
            pltpu.make_async_copy(off_src, off_recv.at[core], off_recv_sem.at[core]).start()

    def chip_of(t):
        turn = CHIPS - 1 - t
        away = jnp.where(turn % 2 == 1, (turn + 1) // 2, CHIPS - turn // 2)
        return (z + away) % CHIPS

    def send_white(phase, t):
        chip = chip_of(t)
        remote = jnp.logical_or(chip != z, zh != core)

        @pl.when(remote)
        def _():
            if phase > 0:
                white_copy(phase - 1, chip).wait_send()
            white_copy(phase, chip).start()

        @pl.when(jnp.logical_not(remote))
        def _():
            white_local(phase).start()

    for phase in range(PHASES):
        def send_one(t, _):
            send_white(phase, t)
            return 0

        lax.fori_loop(0, CHIPS, send_one, 0)

    for block in range(2):
        pltpu.make_async_copy(off_src, off_recv.at[block], off_recv_sem.at[block]).wait()
        move = pltpu.make_async_copy(off_recv.at[block], off_smem.at[block], off_local_sem.at[block])
        move.start()
        move.wait()

    inside = (chain != chains - 1).astype(jnp.float32)
    turned = identity()
    summed = selector()

    def res_copy(phase, block, g):
        return pltpu.make_async_remote_copy(
            src_ref=res_send.at[phase, block, g], dst_ref=res_recv.at[phase, z],
            send_sem=res_send_sem.at[phase, block, g], recv_sem=res_recv_sem.at[phase, z],
            device_id=on_line(core * SEGS + g, block), device_id_type=MESH)

    def res_is_remote(block, g):
        return jnp.logical_or(core * SEGS + g != z, block != core)

    def transposed(rows):
        return lax.dot_general(turned, rows.reshape(SEGS * ROWS, C), BOTH_MINOR, preferred_element_type=jnp.float32)

    for phase in range(PHASES):
        for block in range(2):
            def arrive(s, _):
                white_wait(phase, block, s)
                if block == 0:
                    rim_copy(phase, s).start()
                return 0

            lax.fori_loop(0, SEGS, arrive, 0)
            for part in range(2):
                flipped = transposed(recv[phase, block, part])
                far[part, block * C:(block + 1) * C] = flipped
                own[part, block * C:(block + 1) * C] = flipped.astype(jnp.bfloat16)

        for block in range(2):
            if block == 1:
                def take_rim(s, _):
                    rim_copy(phase, s).wait_recv()
                    return 0

                lax.fori_loop(0, SEGS, take_rim, 0)
                for part in range(2):
                    far[part, 2 * C:3 * C] = transposed(rim[phase, part]) * inside

            def slots(group, _):
                offs = [jnp.clip(off_smem[block, 0, GROUP * group + j], 1, C) for j in range(GROUP)]
                for low in range(0, C, STEP):
                    own_re = own[0, block * C + low:block * C + low + STEP]
                    own_im = own[1, block * C + low:block * C + low + STEP]
                    for j in range(GROUP):
                        rows = pl.ds(block * C + low + offs[j], STEP)
                        far_re = far[0, rows, :].astype(jnp.bfloat16)
                        far_im = far[1, rows, :].astype(jnp.bfloat16)
                        prod[j * C + low:j * C + low + STEP, 0:LANES] = own_re * far_re + own_im * far_im
                        prod[j * C + low:j * C + low + STEP, LANES:2 * LANES] = own_im * far_re - own_re * far_im
                sums = lax.dot_general(summed, prod[...], BOTH_MINOR, preferred_element_type=jnp.float32)
                for i in range(GROUP // 2):
                    g = group * (GROUP // 2) + i
                    pair = [sums[:, (2 * i + j) * C:(2 * i + j + 1) * C] for j in range(2)]
                    res_send[phase, block, g] = jnp.concatenate(pair, axis=0).astype(jnp.bfloat16)

                    @pl.when(res_is_remote(block, g))
                    def _():
                        res_copy(phase, block, g).start()

                    @pl.when(jnp.logical_not(res_is_remote(block, g)))
                    def _():
                        pltpu.make_async_copy(
                            res_send.at[phase, block, g], res_recv.at[phase, z], res_recv_sem.at[phase, z]).start()
                return 0

            lax.fori_loop(0, K // GROUP, slots, 0)

    def finish(chip, _):
        for phase in range(PHASES):
            pltpu.make_async_copy(
                res_send.at[phase, 0, 0], res_recv.at[phase, chip], res_recv_sem.at[phase, chip]).wait()
        return 0

    lax.fori_loop(0, CHIPS, finish, 0)
    whole = res_recv[...].astype(jnp.float32).reshape(PHASES * CHIPS, 2, 2 * BINS, C)
    for j in range(2):
        sums = whole[:, j].reshape(2 * NF, C).astype(jnp.bfloat16)
        out_ref[j] = lax.dot_general(sums, lag_ref[...], (((0,), (0,)), ((), ())),
                                     preferred_element_type=jnp.float32).astype(jnp.bfloat16)

    def drain(t, _):
        @pl.when(jnp.logical_or(t != z, zh != core))
        def _():
            white_copy(PHASES - 1, t).wait_send()
        return 0

    lax.fori_loop(0, CHIPS, drain, 0)

    def drain_more(s, _):
        for phase in range(PHASES):
            rim_copy(phase, s).wait_send()
            for block in range(2):
                @pl.when(res_is_remote(block, s))
                def _():
                    res_copy(phase, block, s).wait_send()
        return 0

    lax.fori_loop(0, SEGS, drain_more, 0)
    for half in range(2):
        @pl.when(off_is_remote(half))
        def _():
            off_copy(half).wait_send()


def shards(columns, records, alive, offsets):
    vmem = pl.BlockSpec(memory_space=pltpu.VMEM)
    rec = jnp.transpose(records[0], (1, 0, 2))
    dma = pltpu.SemaphoreType.DMA
    call = pl.pallas_call(
        functools.partial(kernel, columns),
        out_shape=jax.ShapeDtypeStruct((2, C, NL), jnp.bfloat16),
        in_specs=[vmem] * 5,
        out_specs=vmem,
        scratch_shapes=[
            pltpu.VMEM((W, PHASES * CHIPS, 2 * BINS, C), jnp.float32),
            pltpu.VMEM((PHASES, CHIPS, 2, ROWS, C), jnp.bfloat16),
            pltpu.VMEM((PHASES, 2, 2, SEGS, ROWS, C), jnp.bfloat16),
            pltpu.VMEM((PHASES, 2, SEGS, ROWS, C), jnp.bfloat16),
            pltpu.VMEM((2, 3 * C, LANES), jnp.float32),
            pltpu.VMEM((2, 2 * C, LANES), jnp.bfloat16),
            pltpu.VMEM((GROUP * C, 2 * LANES), jnp.bfloat16),
            pltpu.VMEM((PHASES, 2, SEGS, 4 * BINS, C), jnp.bfloat16),
            pltpu.VMEM((PHASES, CHIPS, 4 * BINS, C), jnp.bfloat16),
            pltpu.VMEM((8, LANES), jnp.int32),
            pltpu.VMEM((2, 8, LANES), jnp.int32),
            pltpu.SMEM((2, 8, LANES), jnp.int32),
            dma((PHASES, CHIPS)),
            dma((PHASES, 2, SEGS)),
            dma((PHASES, SEGS)),
            dma((PHASES, SEGS)),
            dma((PHASES, 2, SEGS)),
            dma((PHASES, CHIPS)),
            dma((2,)),
            dma((2,)),
            dma((2,)),
        ],
        compiler_params=pltpu.CompilerParams(
            collective_id=0, has_side_effects=True, vmem_limit_bytes=32 * 1024 * 1024),
        cost_estimate=pl.CostEstimate(flops=400_000_000, bytes_accessed=3_000_000, transcendentals=1024),
        name="line_correlate",
    )
    return call(rec, alive.reshape(1, C), offsets, forward_table(), lag_table())


def solution(mesh):
    in_specs = (P("seg", "chan", None, None), P("chan"), P("chan", None))
    out_specs = P("seg", "chan", None)
    body = functools.partial(shards, mesh.shape["chan"] // 4)
    return jax.shard_map(body, mesh=mesh, in_specs=in_specs, out_specs=out_specs, check_vma=False)
```

```python
import functools

import jax
import jax.numpy as jnp
import numpy as np
from jax import lax
from jax.experimental import pallas as pl
from jax.experimental.pallas import tpu as pltpu
from jax.sharding import PartitionSpec as P

W = 4
WIN = 512
NF = 128
F0 = 1
NL = 256
K = 16
C = 256
SEGS = 8
CHIPS = 16
PHASES = 2
BINS = NF // CHIPS // PHASES
ROWS = W * BINS
LANES = 128
GROUP = 8
STEP = 32
eps = 1e-06
MESH = pl.DeviceIdType.MESH
BOTH_MINOR = (((1,), (1,)), ((), ()))


def bin_order():
    phase, chip, part, which = np.meshgrid(
        np.arange(PHASES), np.arange(CHIPS), np.arange(2), np.arange(BINS), indexing="ij")
    return (F0 + (chip * PHASES + phase) * BINS + which).reshape(-1), part.reshape(-1)


def forward_table():
    bins, part = bin_order()
    turn = (bins[:, None] * np.arange(WIN)[None, :]) % WIN
    angle = turn * (2.0 * np.pi / WIN)
    rows = np.where(part[:, None] == 0, np.cos(angle), -np.sin(angle))
    return jnp.asarray(rows.astype(np.float32))


def lag_table():
    bins, part = bin_order()
    turn = (bins[:, None] * (np.arange(NL)[None, :] - NL // 2)) % WIN
    angle = turn * (2.0 * np.pi / WIN)
    rows = np.where(part[:, None] == 0, np.cos(angle), -np.sin(angle)) / NF
    return jnp.asarray(rows.astype(np.float32))


def identity():
    row = lax.broadcasted_iota(jnp.int32, (C, C), 0)
    column = lax.broadcasted_iota(jnp.int32, (C, C), 1)
    return (row == column).astype(jnp.float32).astype(jnp.bfloat16)


def selector():
    row = lax.broadcasted_iota(jnp.int32, (2 * BINS, 2 * LANES), 0)
    lane = lax.broadcasted_iota(jnp.int32, (2 * BINS, 2 * LANES), 1)
    same = jnp.logical_and(row % BINS == lane % BINS, row // BINS == lane // LANES)
    return same.astype(jnp.float32).astype(jnp.bfloat16)


def kernel(columns, rec_hbm, alive_hbm, off_hbm, tab_hbm, lag_hbm, out_ref,
           rec_ref, alive_ref, off_ref, tab_ref, lag_ref, raw, send, recv, rim, far, own, prod, res_send, res_recv, off_src, off_recv, off_smem,
           send_sem, recv_sem, rim_send_sem, rim_recv_sem, res_send_sem, res_recv_sem,
           off_send_sem, off_recv_sem, off_local_sem, load_sem):
    chan = lax.axis_index("chan")
    seg = lax.axis_index("seg")
    core = chan % 2
    zh = (chan // 2) % 2
    col = chan // 4
    z = zh * SEGS + seg
    chain = col * 2 + core
    chains = columns * 2
    before = (chain + chains - 1) % chains
    after = (chain + 1) % chains

    def on_line(chip, which):
        return ((col * 2 + chip // SEGS) * 2 + which, chip % SEGS)

    def on_chain(link):
        return (((link // 2) * 2 + zh) * 2 + link % 2, seg)

    barrier = pltpu.get_barrier_semaphore()

    def greet(t, _):
        which = t % 2
        other = core * SEGS + t // 2

        @pl.when(jnp.logical_or(other != z, which != core))
        def _():
            pl.semaphore_signal(barrier, 1, device_id=on_line(other, which), device_id_type=MESH)
        return 0

    lax.fori_loop(0, 2 * SEGS, greet, 0)
    pl.semaphore_signal(barrier, 1, device_id=on_chain(after), device_id_type=MESH)

    loads = [pltpu.make_async_copy(source, target, load_sem.at[i]) for i, (source, target) in enumerate((
        (rec_hbm, rec_ref), (tab_hbm, tab_ref), (alive_hbm, alive_ref), (off_hbm, off_ref), (lag_hbm, lag_ref)))]
    for load in loads:
        load.start()
    for load in loads:
        load.wait()
    off_src[...] = jnp.zeros_like(off_src)
    off_src[0:1, 0:K] = off_ref[...]
    live = alive_ref[...].astype(jnp.float32)

    def white_copy(phase, chip):
        return pltpu.make_async_remote_copy(
            src_ref=send.at[phase, chip], dst_ref=recv.at[phase, core, :, seg],
            send_sem=send_sem.at[phase, chip], recv_sem=recv_sem.at[phase, core, seg],
            device_id=on_line(chip, zh), device_id_type=MESH)

    def white_local(phase):
        return pltpu.make_async_copy(
            send.at[phase, z], recv.at[phase, core, :, seg], recv_sem.at[phase, core, seg])

    def white_wait(phase, block, s):
        pltpu.make_async_copy(
            send.at[phase, 0], recv.at[phase, block, :, s], recv_sem.at[phase, block, s]).wait()

    def rim_copy(phase, s):
        return pltpu.make_async_remote_copy(
            src_ref=recv.at[phase, 0, :, s], dst_ref=rim.at[phase, :, s],
            send_sem=rim_send_sem.at[phase, s], recv_sem=rim_recv_sem.at[phase, s],
            device_id=on_chain(before), device_id_type=MESH)

    def off_copy(half):
        return pltpu.make_async_remote_copy(
            src_ref=off_src, dst_ref=off_recv.at[core],
            send_sem=off_send_sem.at[half], recv_sem=off_recv_sem.at[core],
            device_id=on_line(half * SEGS + seg, zh), device_id_type=MESH)

    def off_is_remote(half):
        return jnp.logical_or(half != zh, zh != core)

    table = tab_ref[...].astype(jnp.bfloat16)
    by_window = jnp.swapaxes(rec_ref[0], 0, 1)
    scales = []
    for w in range(W):
        spectra = lax.dot_general(table, by_window[w], BOTH_MINOR, preferred_element_type=jnp.float32)
        power = jnp.sum(spectra * spectra, axis=0, keepdims=True) * (1.0 / (2 * NF))
        scales.append((lax.rsqrt(power + eps) * live).reshape(1, 1, C))
        raw[w] = spectra.reshape(PHASES * CHIPS, 2 * BINS, C)
    upper = lax.broadcasted_iota(jnp.int32, (1, 2 * BINS, C), 1) < BINS
    some = 4
    for phase in range(PHASES):
        for first in range(0, CHIPS, some):
            real, imag = [], []
            for w in range(0, W, 2):
                at = slice(phase * CHIPS + first, phase * CHIPS + first + some)
                one, two = raw[w, at] * scales[w], raw[w + 1, at] * scales[w + 1]
                real.append(jnp.where(upper, one, pltpu.roll(two, BINS, 1)))
                imag.append(jnp.where(upper, pltpu.roll(one, BINS, 1), two))
            for part, rows in enumerate((real, imag)):
                send[phase, first:first + some, part] = jnp.concatenate(rows, axis=1).astype(jnp.bfloat16)

    met = CHIPS + 1 - (zh == core).astype(jnp.int32)
    pl.semaphore_wait(barrier, met)
    for half in range(2):
        @pl.when(off_is_remote(half))
        def _():
            off_copy(half).start()

        @pl.when(jnp.logical_not(off_is_remote(half)))
        def _():
            pltpu.make_async_copy(off_src, off_recv.at[core], off_recv_sem.at[core]).start()

    def away(t):
        turn = CHIPS - 1 - t
        return jnp.where(turn % 2 == 1, (turn + 1) // 2, CHIPS - turn // 2)

    def send_white(phase, t):
        chip = (z + away(t)) % CHIPS
        remote = jnp.logical_or(chip != z, zh != core)

        @pl.when(remote)
        def _():
            if phase > 0:
                white_copy(phase - 1, chip).wait_send()
            white_copy(phase, chip).start()

        @pl.when(jnp.logical_not(remote))
        def _():
            white_local(phase).start()

    for phase in range(PHASES):
        def send_one(t, _):
            send_white(phase, t)
            return 0

        lax.fori_loop(0, CHIPS, send_one, 0)

    for block in range(2):
        pltpu.make_async_copy(off_src, off_recv.at[block], off_recv_sem.at[block]).wait()
        move = pltpu.make_async_copy(off_recv.at[block], off_smem.at[block], off_local_sem.at[block])
        move.start()
        move.wait()

    inside = (chain != chains - 1).astype(jnp.float32)
    turned = identity()
    summed = selector()

    def res_copy(phase, block, g):
        return pltpu.make_async_remote_copy(
            src_ref=res_send.at[phase, block, g], dst_ref=res_recv.at[phase, z],
            send_sem=res_send_sem.at[phase, block, g], recv_sem=res_recv_sem.at[phase, z],
            device_id=on_line(core * SEGS + g, block), device_id_type=MESH)

    def res_is_remote(block, g):
        return jnp.logical_or(core * SEGS + g != z, block != core)

    def transposed(rows):
        return lax.dot_general(turned, rows.reshape(SEGS * ROWS, C), BOTH_MINOR, preferred_element_type=jnp.float32)

    for phase in range(PHASES):
        def arrive(t, _):
            chip = (z + CHIPS - away(t)) % CHIPS

            @pl.when(chip // SEGS == core)
            def _():
                s = chip % SEGS
                white_wait(phase, 0, s)
                rim_copy(phase, s).start()
                white_wait(phase, 1, s)
            return 0

        lax.fori_loop(0, CHIPS, arrive, 0)
        for block in range(2):
            for part in range(2):
                flipped = transposed(recv[phase, block, part])
                far[part, block * C:(block + 1) * C] = flipped
                own[part, block * C:(block + 1) * C] = flipped.astype(jnp.bfloat16)

        for block in range(2):
            if block == 1:
                def take_rim(s, _):
                    rim_copy(phase, s).wait_recv()
                    return 0

                lax.fori_loop(0, SEGS, take_rim, 0)
                for part in range(2):
                    far[part, 2 * C:3 * C] = transposed(rim[phase, part]) * inside

            def slots(group, _):
                offs = [jnp.clip(off_smem[block, 0, GROUP * group + j], 1, C) for j in range(GROUP)]
                for low in range(0, C, STEP):
                    own_re = own[0, block * C + low:block * C + low + STEP]
                    own_im = own[1, block * C + low:block * C + low + STEP]
                    for j in range(GROUP):
                        rows = pl.ds(block * C + low + offs[j], STEP)
                        far_re = far[0, rows, :].astype(jnp.bfloat16)
                        far_im = far[1, rows, :].astype(jnp.bfloat16)
                        prod[j * C + low:j * C + low + STEP, 0:LANES] = own_re * far_re + own_im * far_im
                        prod[j * C + low:j * C + low + STEP, LANES:2 * LANES] = own_im * far_re - own_re * far_im
                sums = lax.dot_general(summed, prod[...], BOTH_MINOR, preferred_element_type=jnp.float32)
                for i in range(GROUP // 2):
                    g = group * (GROUP // 2) + i
                    pair = [sums[:, (2 * i + j) * C:(2 * i + j + 1) * C] for j in range(2)]
                    res_send[phase, block, g] = jnp.concatenate(pair, axis=0).astype(jnp.bfloat16)

                    @pl.when(res_is_remote(block, g))
                    def _():
                        res_copy(phase, block, g).start()

                    @pl.when(jnp.logical_not(res_is_remote(block, g)))
                    def _():
                        pltpu.make_async_copy(
                            res_send.at[phase, block, g], res_recv.at[phase, z], res_recv_sem.at[phase, z]).start()
                return 0

            lax.fori_loop(0, K // GROUP, slots, 0)

    lags = lag_ref[...].astype(jnp.bfloat16)
    result = [0.0, 0.0]
    for phase in range(PHASES):
        def finish(chip, _):
            pltpu.make_async_copy(
                res_send.at[phase, 0, 0], res_recv.at[phase, chip], res_recv_sem.at[phase, chip]).wait()
            return 0

        lax.fori_loop(0, CHIPS, finish, 0)
        whole = res_recv[phase].astype(jnp.float32).reshape(CHIPS, 2, 2 * BINS, C)
        rows = slice(phase * CHIPS * 2 * BINS, (phase + 1) * CHIPS * 2 * BINS)
        for j in range(2):
            sums = whole[:, j].reshape(CHIPS * 2 * BINS, C).astype(jnp.bfloat16)
            result[j] += lax.dot_general(sums, lags[rows], (((0,), (0,)), ((), ())),
                                         preferred_element_type=jnp.float32)
    for j in range(2):
        out_ref[j] = result[j].astype(jnp.bfloat16)

    def drain(t, _):
        @pl.when(jnp.logical_or(t != z, zh != core))
        def _():
            white_copy(PHASES - 1, t).wait_send()
        return 0

    lax.fori_loop(0, CHIPS, drain, 0)

    def drain_more(s, _):
        for phase in range(PHASES):
            rim_copy(phase, s).wait_send()
            for block in range(2):
                @pl.when(res_is_remote(block, s))
                def _():
                    res_copy(phase, block, s).wait_send()
        return 0

    lax.fori_loop(0, SEGS, drain_more, 0)
    for half in range(2):
        @pl.when(off_is_remote(half))
        def _():
            off_copy(half).wait_send()


def shards(columns, records, alive, offsets):
    vmem = pl.BlockSpec(memory_space=pltpu.VMEM)
    dma = pltpu.SemaphoreType.DMA
    call = pl.pallas_call(
        functools.partial(kernel, columns),
        out_shape=jax.ShapeDtypeStruct((2, C, NL), jnp.bfloat16),
        in_specs=[pl.BlockSpec(memory_space=pltpu.HBM)] * 5,
        out_specs=vmem,
        scratch_shapes=[
            pltpu.VMEM((1, C, W, WIN), jnp.bfloat16),
            pltpu.VMEM((1, C), jnp.int32),
            pltpu.VMEM((1, K), jnp.int32),
            pltpu.VMEM((2 * NF, WIN), jnp.float32),
            pltpu.VMEM((2 * NF, NL), jnp.float32),
            pltpu.VMEM((W, PHASES * CHIPS, 2 * BINS, C), jnp.float32),
            pltpu.VMEM((PHASES, CHIPS, 2, ROWS, C), jnp.bfloat16),
            pltpu.VMEM((PHASES, 2, 2, SEGS, ROWS, C), jnp.bfloat16),
            pltpu.VMEM((PHASES, 2, SEGS, ROWS, C), jnp.bfloat16),
            pltpu.VMEM((2, 3 * C, LANES), jnp.float32),
            pltpu.VMEM((2, 2 * C, LANES), jnp.bfloat16),
            pltpu.VMEM((GROUP * C, 2 * LANES), jnp.bfloat16),
            pltpu.VMEM((PHASES, 2, SEGS, 4 * BINS, C), jnp.bfloat16),
            pltpu.VMEM((PHASES, CHIPS, 4 * BINS, C), jnp.bfloat16),
            pltpu.VMEM((8, LANES), jnp.int32),
            pltpu.VMEM((2, 8, LANES), jnp.int32),
            pltpu.SMEM((2, 8, LANES), jnp.int32),
            dma((PHASES, CHIPS)),
            dma((PHASES, 2, SEGS)),
            dma((PHASES, SEGS)),
            dma((PHASES, SEGS)),
            dma((PHASES, 2, SEGS)),
            dma((PHASES, CHIPS)),
            dma((2,)),
            dma((2,)),
            dma((2,)),
            dma((5,)),
        ],
        compiler_params=pltpu.CompilerParams(
            collective_id=0, has_side_effects=True, vmem_limit_bytes=56 * 1024 * 1024),
        cost_estimate=pl.CostEstimate(flops=400_000_000, bytes_accessed=3_000_000, transcendentals=1024),
        name="line_correlate",
    )
    return call(records, alive.reshape(1, C), offsets, forward_table(), lag_table())


def solution(mesh):
    in_specs = (P("seg", "chan", None, None), P("chan"), P("chan", None))
    out_specs = P("seg", "chan", None)
    body = functools.partial(shards, mesh.shape["chan"] // 4)
    return jax.shard_map(body, mesh=mesh, in_specs=in_specs, out_specs=out_specs, check_vma=False)
```

```python
import functools

import jax
import jax.numpy as jnp
import numpy as np
from jax import lax
from jax.experimental import pallas as pl
from jax.experimental.pallas import tpu as pltpu
from jax.sharding import PartitionSpec as P

W = 4
WIN = 512
NF = 128
F0 = 1
NL = 256
K = 16
C = 256
SEGS = 8
CHIPS = 16
PHASES = 2
BINS = NF // CHIPS // PHASES
ROWS = W * BINS
LANES = 128
GROUP = 8
STEP = 32
eps = 1e-06
MESH = pl.DeviceIdType.MESH
BOTH_MINOR = (((1,), (1,)), ((), ()))


def bin_order():
    phase, chip, part, which = np.meshgrid(
        np.arange(PHASES), np.arange(CHIPS), np.arange(2), np.arange(BINS), indexing="ij")
    return (F0 + (chip * PHASES + phase) * BINS + which).reshape(-1), part.reshape(-1)


def tables():
    bins, part = bin_order()

    def rows(times):
        angle = ((bins[:, None] * times[None, :]) % WIN) * (2.0 * np.pi / WIN)
        return np.where(part[:, None] == 0, np.cos(angle), -np.sin(angle))

    both = np.concatenate([rows(np.arange(WIN)), rows(np.arange(NL) - NL // 2) / NF], axis=1)
    return jnp.asarray(both.astype(np.float32))


def identity():
    row = lax.broadcasted_iota(jnp.int32, (C, C), 0)
    column = lax.broadcasted_iota(jnp.int32, (C, C), 1)
    return (row == column).astype(jnp.float32).astype(jnp.bfloat16)


def selector():
    row = lax.broadcasted_iota(jnp.int32, (2 * BINS, 2 * LANES), 0)
    lane = lax.broadcasted_iota(jnp.int32, (2 * BINS, 2 * LANES), 1)
    same = jnp.logical_and(row % BINS == lane % BINS, row // BINS == lane // LANES)
    return same.astype(jnp.float32).astype(jnp.bfloat16)


def kernel(columns, rec_hbm, alive_hbm, off_hbm, tab_hbm, out_ref,
           rec_ref, alive_ref, off_ref, tab_ref, raw, send, recv, rim, far, own, prod, res_send, res_recv, off_src, off_recv, off_smem,
           send_sem, recv_sem, rim_send_sem, rim_recv_sem, res_send_sem, res_recv_sem,
           off_send_sem, off_recv_sem, off_local_sem, load_sem):
    chan = lax.axis_index("chan")
    seg = lax.axis_index("seg")
    core = chan % 2
    zh = (chan // 2) % 2
    col = chan // 4
    z = zh * SEGS + seg
    chain = col * 2 + core
    chains = columns * 2
    before = (chain + chains - 1) % chains
    after = (chain + 1) % chains

    def on_line(chip, which):
        return ((col * 2 + chip // SEGS) * 2 + which, chip % SEGS)

    def on_chain(link):
        return (((link // 2) * 2 + zh) * 2 + link % 2, seg)

    barrier = pltpu.get_barrier_semaphore()

    for s in range(SEGS):
        for which in range(2):
            sender = ((col * 2 + core) * 2 + which, s)

            @pl.when(jnp.logical_or(sender[0] != chan, s != seg))
            def _():
                pl.semaphore_signal(barrier, 1, device_id=sender, device_id_type=MESH)
    pl.semaphore_signal(barrier, 1, device_id=on_chain(after), device_id_type=MESH)

    loads = [pltpu.make_async_copy(source, target, load_sem.at[i]) for i, (source, target) in enumerate((
        (rec_hbm, rec_ref), (tab_hbm, tab_ref), (alive_hbm, alive_ref), (off_hbm, off_ref)))]
    for load in loads:
        load.start()
    for load in loads:
        load.wait()
    off_src[...] = jnp.zeros_like(off_src)
    off_src[0:1, 0:K] = off_ref[...]
    live = alive_ref[...].astype(jnp.float32)

    def white_copy(phase, chip):
        return pltpu.make_async_remote_copy(
            src_ref=send.at[phase, chip], dst_ref=recv.at[phase, core, :, seg],
            send_sem=send_sem.at[phase, chip], recv_sem=recv_sem.at[phase, core, seg],
            device_id=on_line(chip, zh), device_id_type=MESH)

    def white_local(phase):
        return pltpu.make_async_copy(
            send.at[phase, z], recv.at[phase, core, :, seg], recv_sem.at[phase, core, seg])

    def white_wait(phase, block, s):
        pltpu.make_async_copy(
            send.at[phase, 0], recv.at[phase, block, :, s], recv_sem.at[phase, block, s]).wait()

    def rim_copy(phase, s):
        return pltpu.make_async_remote_copy(
            src_ref=recv.at[phase, 0, :, s], dst_ref=rim.at[phase, :, s],
            send_sem=rim_send_sem.at[phase, s], recv_sem=rim_recv_sem.at[phase, s],
            device_id=on_chain(before), device_id_type=MESH)

    def off_copy(half):
        return pltpu.make_async_remote_copy(
            src_ref=off_src, dst_ref=off_recv.at[core],
            send_sem=off_send_sem.at[half], recv_sem=off_recv_sem.at[core],
            device_id=on_line(half * SEGS + seg, zh), device_id_type=MESH)

    def off_is_remote(half):
        return jnp.logical_or(half != zh, zh != core)

    table = tab_ref[:, :WIN].astype(jnp.bfloat16)
    by_window = jnp.swapaxes(rec_ref[0], 0, 1)
    scales = []
    for w in range(W):
        spectra = lax.dot_general(table, by_window[w], BOTH_MINOR, preferred_element_type=jnp.float32)
        power = jnp.sum(spectra * spectra, axis=0, keepdims=True) * (1.0 / (2 * NF))
        scales.append((lax.rsqrt(power + eps) * live).reshape(1, 1, C))
        raw[w] = spectra.reshape(PHASES * CHIPS, 2 * BINS, C)
    upper = lax.broadcasted_iota(jnp.int32, (1, 2 * BINS, C), 1) < BINS
    some = 4
    for phase in range(PHASES):
        for first in range(0, CHIPS, some):
            real, imag = [], []
            for w in range(0, W, 2):
                at = slice(phase * CHIPS + first, phase * CHIPS + first + some)
                one, two = raw[w, at] * scales[w], raw[w + 1, at] * scales[w + 1]
                real.append(jnp.where(upper, one, pltpu.roll(two, BINS, 1)))
                imag.append(jnp.where(upper, pltpu.roll(one, BINS, 1), two))
            for part, rows in enumerate((real, imag)):
                send[phase, first:first + some, part] = jnp.concatenate(rows, axis=1).astype(jnp.bfloat16)

    met = CHIPS + 1 - (zh == core).astype(jnp.int32)
    pl.semaphore_wait(barrier, met)
    for half in range(2):
        @pl.when(off_is_remote(half))
        def _():
            off_copy(half).start()

        @pl.when(jnp.logical_not(off_is_remote(half)))
        def _():
            pltpu.make_async_copy(off_src, off_recv.at[core], off_recv_sem.at[core]).start()

    def away(t):
        turn = CHIPS - 1 - t
        return jnp.where(turn % 2 == 1, (turn + 1) // 2, CHIPS - turn // 2)

    def send_white(phase, t):
        chip = (z + away(t)) % CHIPS
        remote = jnp.logical_or(chip != z, zh != core)

        @pl.when(remote)
        def _():
            if phase > 0:
                white_copy(phase - 1, chip).wait_send()
            white_copy(phase, chip).start()

        @pl.when(jnp.logical_not(remote))
        def _():
            white_local(phase).start()

    for phase in range(PHASES):
        def send_one(t, _):
            send_white(phase, t)
            return 0

        lax.fori_loop(0, CHIPS, send_one, 0)

    for block in range(2):
        pltpu.make_async_copy(off_src, off_recv.at[block], off_recv_sem.at[block]).wait()
        move = pltpu.make_async_copy(off_recv.at[block], off_smem.at[block], off_local_sem.at[block])
        move.start()
        move.wait()

    inside = (chain != chains - 1).astype(jnp.float32)
    turned = identity()
    summed = selector()

    def res_copy(phase, block, g):
        return pltpu.make_async_remote_copy(
            src_ref=res_send.at[phase, block, g], dst_ref=res_recv.at[phase, z],
            send_sem=res_send_sem.at[phase, block, g], recv_sem=res_recv_sem.at[phase, z],
            device_id=on_line(core * SEGS + g, block), device_id_type=MESH)

    def res_is_remote(block, g):
        return jnp.logical_or(core * SEGS + g != z, block != core)

    def send_sums(phase, block, g):
        remote = res_is_remote(block, g)

        @pl.when(remote)
        def _():
            res_copy(phase, block, g).start()

        @pl.when(jnp.logical_not(remote))
        def _():
            pltpu.make_async_copy(
                res_send.at[phase, block, g], res_recv.at[phase, z], res_recv_sem.at[phase, z]).start()

    def transposed(rows):
        return lax.dot_general(turned, rows.reshape(SEGS * ROWS, C), BOTH_MINOR, preferred_element_type=jnp.float32)

    for phase in range(PHASES):
        def arrive(t, _):
            chip = (z + CHIPS - away(t)) % CHIPS

            @pl.when(chip // SEGS == core)
            def _():
                s = chip % SEGS
                white_wait(phase, 0, s)
                rim_copy(phase, s).start()
                white_wait(phase, 1, s)
            return 0

        lax.fori_loop(0, CHIPS, arrive, 0)
        for block in range(2):
            for part in range(2):
                flipped = transposed(recv[phase, block, part])
                far[part, block * C:(block + 1) * C] = flipped
                own[part, block * C:(block + 1) * C] = flipped.astype(jnp.bfloat16)

        def one_group(block, group):
            offs = [jnp.clip(off_smem[block, 0, GROUP * group + j], 1, C) for j in range(GROUP)]
            for low in range(0, C, STEP):
                own_re = own[0, block * C + low:block * C + low + STEP]
                own_im = own[1, block * C + low:block * C + low + STEP]
                for j in range(GROUP):
                    rows = pl.ds(block * C + low + offs[j], STEP)
                    far_re = far[0, rows, :].astype(jnp.bfloat16)
                    far_im = far[1, rows, :].astype(jnp.bfloat16)
                    prod[j * C + low:j * C + low + STEP, 0:LANES] = own_re * far_re + own_im * far_im
                    prod[j * C + low:j * C + low + STEP, LANES:2 * LANES] = own_im * far_re - own_re * far_im
            sums = lax.dot_general(summed, prod[...], BOTH_MINOR, preferred_element_type=jnp.float32)
            for i in range(GROUP // 2):
                g = group * (GROUP // 2) + i
                pair = [sums[:, (2 * i + j) * C:(2 * i + j + 1) * C] for j in range(2)]
                res_send[phase, block, g] = jnp.concatenate(pair, axis=0).astype(jnp.bfloat16)
                send_sums(phase, block, g)

        def both_blocks(group, _):
            one_group(0, group)
            if_rim(group)
            one_group(1, group)
            return 0

        def if_rim(group):
            @pl.when(group == 0)
            def _():
                def take_rim(s, _):
                    rim_copy(phase, s).wait_recv()
                    return 0

                lax.fori_loop(0, SEGS, take_rim, 0)
                for part in range(2):
                    far[part, 2 * C:3 * C] = transposed(rim[phase, part]) * inside

        lax.fori_loop(0, K // GROUP, both_blocks, 0)
    lags = tab_ref[:, WIN:].astype(jnp.bfloat16)
    result = [0.0, 0.0]
    for phase in range(PHASES):
        def finish(chip, _):
            pltpu.make_async_copy(
                res_send.at[phase, 0, 0], res_recv.at[phase, chip], res_recv_sem.at[phase, chip]).wait()
            return 0

        lax.fori_loop(0, CHIPS, finish, 0)
        whole = res_recv[phase].astype(jnp.float32).reshape(CHIPS, 2, 2 * BINS, C)
        rows = slice(phase * CHIPS * 2 * BINS, (phase + 1) * CHIPS * 2 * BINS)
        for j in range(2):
            sums = whole[:, j].reshape(CHIPS * 2 * BINS, C).astype(jnp.bfloat16)
            result[j] += lax.dot_general(sums, lags[rows], (((0,), (0,)), ((), ())),
                                         preferred_element_type=jnp.float32)
    for j in range(2):
        out_ref[j] = result[j].astype(jnp.bfloat16)

    def drain(t, _):
        @pl.when(jnp.logical_or(t != z, zh != core))
        def _():
            white_copy(PHASES - 1, t).wait_send()
        return 0

    lax.fori_loop(0, CHIPS, drain, 0)

    def drain_more(s, _):
        for phase in range(PHASES):
            rim_copy(phase, s).wait_send()
            for block in range(2):
                @pl.when(res_is_remote(block, s))
                def _():
                    res_copy(phase, block, s).wait_send()
        return 0

    lax.fori_loop(0, SEGS, drain_more, 0)
    for half in range(2):
        @pl.when(off_is_remote(half))
        def _():
            off_copy(half).wait_send()


def shards(columns, records, alive, offsets):
    vmem = pl.BlockSpec(memory_space=pltpu.VMEM)
    dma = pltpu.SemaphoreType.DMA
    call = pl.pallas_call(
        functools.partial(kernel, columns),
        out_shape=jax.ShapeDtypeStruct((2, C, NL), jnp.bfloat16),
        in_specs=[pl.BlockSpec(memory_space=pltpu.HBM)] * 4,
        out_specs=vmem,
        scratch_shapes=[
            pltpu.VMEM((1, C, W, WIN), jnp.bfloat16),
            pltpu.VMEM((1, C), jnp.int32),
            pltpu.VMEM((1, K), jnp.int32),
            pltpu.VMEM((2 * NF, WIN + NL), jnp.float32),
            pltpu.VMEM((W, PHASES * CHIPS, 2 * BINS, C), jnp.float32),
            pltpu.VMEM((PHASES, CHIPS, 2, ROWS, C), jnp.bfloat16),
            pltpu.VMEM((PHASES, 2, 2, SEGS, ROWS, C), jnp.bfloat16),
            pltpu.VMEM((PHASES, 2, SEGS, ROWS, C), jnp.bfloat16),
            pltpu.VMEM((2, 3 * C, LANES), jnp.float32),
            pltpu.VMEM((2, 2 * C, LANES), jnp.bfloat16),
            pltpu.VMEM((GROUP * C, 2 * LANES), jnp.bfloat16),
            pltpu.VMEM((PHASES, 2, SEGS, 4 * BINS, C), jnp.bfloat16),
            pltpu.VMEM((PHASES, CHIPS, 4 * BINS, C), jnp.bfloat16),
            pltpu.VMEM((8, LANES), jnp.int32),
            pltpu.VMEM((2, 8, LANES), jnp.int32),
            pltpu.SMEM((2, 8, LANES), jnp.int32),
            dma((PHASES, CHIPS)),
            dma((PHASES, 2, SEGS)),
            dma((PHASES, SEGS)),
            dma((PHASES, SEGS)),
            dma((PHASES, 2, SEGS)),
            dma((PHASES, CHIPS)),
            dma((2,)),
            dma((2,)),
            dma((2,)),
            dma((4,)),
        ],
        compiler_params=pltpu.CompilerParams(
            collective_id=0, has_side_effects=True, vmem_limit_bytes=53 * 1024 * 1024),
        cost_estimate=pl.CostEstimate(flops=400_000_000, bytes_accessed=3_000_000, transcendentals=1024),
        name="line_correlate",
    )
    return call(records, alive.reshape(1, C), offsets, tables())


def solution(mesh):
    in_specs = (P("seg", "chan", None, None), P("chan"), P("chan", None))
    out_specs = P("seg", "chan", None)
    body = functools.partial(shards, mesh.shape["chan"] // 4)
    return jax.shard_map(body, mesh=mesh, in_specs=in_specs, out_specs=out_specs, check_vma=False)
```

```python
import functools

import jax
import jax.numpy as jnp
import numpy as np
from jax import lax
from jax.experimental import pallas as pl
from jax.experimental.pallas import tpu as pltpu
from jax.sharding import PartitionSpec as P

W = 4
WIN = 512
NF = 128
F0 = 1
NL = 256
K = 16
C = 256
SEGS = 8
CHIPS = 16
PHASES = 2
BINS = NF // CHIPS // PHASES
ROWS = W * BINS
LANES = 128
GROUP = 8
STEP = 32
eps = 1e-06
MESH = pl.DeviceIdType.MESH
BOTH_MINOR = (((1,), (1,)), ((), ()))


def bin_order():
    phase, chip, part, which = np.meshgrid(
        np.arange(PHASES), np.arange(CHIPS), np.arange(2), np.arange(BINS), indexing="ij")
    return (F0 + (chip * PHASES + phase) * BINS + which).reshape(-1), part.reshape(-1)


def tables():
    bins, part = bin_order()

    def rows(times):
        angle = ((bins[:, None] * times[None, :]) % WIN) * (2.0 * np.pi / WIN)
        return np.where(part[:, None] == 0, np.cos(angle), -np.sin(angle))

    both = np.concatenate([rows(np.arange(WIN)), rows(np.arange(NL) - NL // 2) / NF], axis=1)
    return jnp.asarray(both.astype(np.float32))


def identity():
    row = lax.broadcasted_iota(jnp.int32, (C, C), 0)
    column = lax.broadcasted_iota(jnp.int32, (C, C), 1)
    return (row == column).astype(jnp.float32).astype(jnp.bfloat16)


def selector():
    row = lax.broadcasted_iota(jnp.int32, (2 * BINS, 2 * LANES), 0)
    lane = lax.broadcasted_iota(jnp.int32, (2 * BINS, 2 * LANES), 1)
    same = jnp.logical_and(row % BINS == lane % BINS, row // BINS == lane // LANES)
    return same.astype(jnp.float32).astype(jnp.bfloat16)


def kernel(columns, rec_hbm, alive_hbm, off_hbm, tab_hbm, out_ref,
           rec_ref, alive_ref, off_ref, tab_ref, raw, send, recv, rim, far, own, prod, res_send, res_recv, off_src, off_recv, off_smem,
           send_sem, recv_sem, rim_send_sem, rim_recv_sem, res_send_sem, res_recv_sem,
           off_send_sem, off_recv_sem, off_local_sem, load_sem):
    chan = lax.axis_index("chan")
    seg = lax.axis_index("seg")
    core = chan % 2
    zh = (chan // 2) % 2
    col = chan // 4
    z = zh * SEGS + seg
    chain = col * 2 + core
    chains = columns * 2
    before = (chain + chains - 1) % chains
    after = (chain + 1) % chains

    def on_line(chip, which):
        return ((col * 2 + chip // SEGS) * 2 + which, chip % SEGS)

    def on_chain(link):
        return (((link // 2) * 2 + zh) * 2 + link % 2, seg)

    loads = [pltpu.make_async_copy(source, target, load_sem.at[i]) for i, (source, target) in enumerate((
        (rec_hbm, rec_ref), (tab_hbm, tab_ref), (alive_hbm, alive_ref), (off_hbm, off_ref)))]
    for load in loads:
        load.start()
    barrier = pltpu.get_barrier_semaphore()

    for s in range(SEGS):
        for which in range(2):
            sender = ((col * 2 + core) * 2 + which, s)

            @pl.when(jnp.logical_or(sender[0] != chan, s != seg))
            def _():
                pl.semaphore_signal(barrier, 1, device_id=sender, device_id_type=MESH)
    pl.semaphore_signal(barrier, 1, device_id=on_chain(after), device_id_type=MESH)

    for load in loads:
        load.wait()
    off_src[...] = jnp.zeros_like(off_src)
    off_src[0:1, 0:K] = off_ref[...]
    live = alive_ref[...].astype(jnp.float32)

    def white_copy(phase, chip):
        return pltpu.make_async_remote_copy(
            src_ref=send.at[phase, chip], dst_ref=recv.at[phase, core, :, seg],
            send_sem=send_sem.at[phase, chip], recv_sem=recv_sem.at[phase, core, seg],
            device_id=on_line(chip, zh), device_id_type=MESH)

    def white_local(phase):
        return pltpu.make_async_copy(
            send.at[phase, z], recv.at[phase, core, :, seg], recv_sem.at[phase, core, seg])

    def white_wait(phase, block, s):
        pltpu.make_async_copy(
            send.at[phase, 0], recv.at[phase, block, :, s], recv_sem.at[phase, block, s]).wait()

    def rim_copy(phase, s):
        return pltpu.make_async_remote_copy(
            src_ref=recv.at[phase, 0, :, s], dst_ref=rim.at[phase, :, s],
            send_sem=rim_send_sem.at[phase, s], recv_sem=rim_recv_sem.at[phase, s],
            device_id=on_chain(before), device_id_type=MESH)

    def off_copy(half):
        return pltpu.make_async_remote_copy(
            src_ref=off_src, dst_ref=off_recv.at[core],
            send_sem=off_send_sem.at[half], recv_sem=off_recv_sem.at[core],
            device_id=on_line(half * SEGS + seg, zh), device_id_type=MESH)

    def off_is_remote(half):
        return jnp.logical_or(half != zh, zh != core)

    table = tab_ref[:, :WIN].astype(jnp.bfloat16)
    by_window = jnp.swapaxes(rec_ref[0], 0, 1)
    scales = []
    for w in range(W):
        spectra = lax.dot_general(table, by_window[w], BOTH_MINOR, preferred_element_type=jnp.float32)
        power = jnp.sum(spectra * spectra, axis=0, keepdims=True) * (1.0 / (2 * NF))
        scales.append((lax.rsqrt(power + eps) * live).reshape(1, 1, C))
        raw[w] = spectra.reshape(PHASES * CHIPS, 2 * BINS, C)
    upper = lax.broadcasted_iota(jnp.int32, (1, 2 * BINS, C), 1) < BINS
    some = 4
    for phase in range(PHASES):
        for first in range(0, CHIPS, some):
            real, imag = [], []
            for w in range(0, W, 2):
                at = slice(phase * CHIPS + first, phase * CHIPS + first + some)
                one, two = raw[w, at] * scales[w], raw[w + 1, at] * scales[w + 1]
                real.append(jnp.where(upper, one, pltpu.roll(two, BINS, 1)))
                imag.append(jnp.where(upper, pltpu.roll(one, BINS, 1), two))
            for part, rows in enumerate((real, imag)):
                send[phase, first:first + some, part] = jnp.concatenate(rows, axis=1).astype(jnp.bfloat16)

    met = CHIPS + 1 - (zh == core).astype(jnp.int32)
    pl.semaphore_wait(barrier, met)
    for half in range(2):
        @pl.when(off_is_remote(half))
        def _():
            off_copy(half).start()

        @pl.when(jnp.logical_not(off_is_remote(half)))
        def _():
            pltpu.make_async_copy(off_src, off_recv.at[core], off_recv_sem.at[core]).start()

    def away(t):
        turn = CHIPS - 1 - t
        return jnp.where(turn % 2 == 1, (turn + 1) // 2, CHIPS - turn // 2)

    def send_white(phase, t):
        chip = (z + away(t)) % CHIPS
        remote = jnp.logical_or(chip != z, zh != core)

        @pl.when(remote)
        def _():
            if phase > 0:
                white_copy(phase - 1, chip).wait_send()
            white_copy(phase, chip).start()

        @pl.when(jnp.logical_not(remote))
        def _():
            white_local(phase).start()

    for phase in range(PHASES):
        def send_one(t, _):
            send_white(phase, t)
            return 0

        lax.fori_loop(0, CHIPS, send_one, 0)

    for block in range(2):
        pltpu.make_async_copy(off_src, off_recv.at[block], off_recv_sem.at[block]).wait()
        move = pltpu.make_async_copy(off_recv.at[block], off_smem.at[block], off_local_sem.at[block])
        move.start()
        move.wait()

    inside = (chain != chains - 1).astype(jnp.float32)
    turned = identity()
    summed = selector()

    def res_copy(phase, block, g):
        return pltpu.make_async_remote_copy(
            src_ref=res_send.at[phase, block, g], dst_ref=res_recv.at[phase, z],
            send_sem=res_send_sem.at[phase, block, g], recv_sem=res_recv_sem.at[phase, z],
            device_id=on_line(core * SEGS + g, block), device_id_type=MESH)

    def res_is_remote(block, g):
        return jnp.logical_or(core * SEGS + g != z, block != core)

    def send_sums(phase, block, g):
        remote = res_is_remote(block, g)

        @pl.when(remote)
        def _():
            res_copy(phase, block, g).start()

        @pl.when(jnp.logical_not(remote))
        def _():
            pltpu.make_async_copy(
                res_send.at[phase, block, g], res_recv.at[phase, z], res_recv_sem.at[phase, z]).start()

    def transposed(rows):
        return lax.dot_general(turned, rows.reshape(SEGS * ROWS, C), BOTH_MINOR, preferred_element_type=jnp.float32)

    for phase in range(PHASES):
        def arrive(t, _):
            chip = (z + CHIPS - away(t)) % CHIPS

            @pl.when(chip // SEGS == core)
            def _():
                s = chip % SEGS
                white_wait(phase, 0, s)
                rim_copy(phase, s).start()
            return 0

        lax.fori_loop(0, CHIPS, arrive, 0)

        def arrive_more(s, _):
            white_wait(phase, 1, s)
            return 0

        lax.fori_loop(0, SEGS, arrive_more, 0)
        for block in range(2):
            for part in range(2):
                flipped = transposed(recv[phase, block, part])
                far[part, block * C:(block + 1) * C] = flipped
                own[part, block * C:(block + 1) * C] = flipped.astype(jnp.bfloat16)

        def one_group(block, group):
            offs = [jnp.clip(off_smem[block, 0, GROUP * group + j], 1, C) for j in range(GROUP)]
            for low in range(0, C, STEP):
                own_re = own[0, block * C + low:block * C + low + STEP]
                own_im = own[1, block * C + low:block * C + low + STEP]
                for j in range(GROUP):
                    rows = pl.ds(block * C + low + offs[j], STEP)
                    far_re = far[0, rows, :].astype(jnp.bfloat16)
                    far_im = far[1, rows, :].astype(jnp.bfloat16)
                    prod[j * C + low:j * C + low + STEP, 0:LANES] = own_re * far_re + own_im * far_im
                    prod[j * C + low:j * C + low + STEP, LANES:2 * LANES] = own_im * far_re - own_re * far_im
            sums = lax.dot_general(summed, prod[...], BOTH_MINOR, preferred_element_type=jnp.float32)
            for i in range(GROUP // 2):
                g = group * (GROUP // 2) + i
                pair = [sums[:, (2 * i + j) * C:(2 * i + j + 1) * C] for j in range(2)]
                res_send[phase, block, g] = jnp.concatenate(pair, axis=0).astype(jnp.bfloat16)
                send_sums(phase, block, g)

        def both_blocks(group, _):
            one_group(0, group)
            if_rim(group)
            one_group(1, group)
            return 0

        def if_rim(group):
            @pl.when(group == 0)
            def _():
                def take_rim(s, _):
                    rim_copy(phase, s).wait_recv()
                    return 0

                lax.fori_loop(0, SEGS, take_rim, 0)
                for part in range(2):
                    far[part, 2 * C:3 * C] = transposed(rim[phase, part]) * inside

        lax.fori_loop(0, K // GROUP, both_blocks, 0)
    lags = tab_ref[:, WIN:].astype(jnp.bfloat16)
    result = [0.0, 0.0]
    for phase in range(PHASES):
        def finish(chip, _):
            pltpu.make_async_copy(
                res_send.at[phase, 0, 0], res_recv.at[phase, chip], res_recv_sem.at[phase, chip]).wait()
            return 0

        lax.fori_loop(0, CHIPS, finish, 0)
        whole = res_recv[phase].astype(jnp.float32).reshape(CHIPS, 2, 2 * BINS, C)
        rows = slice(phase * CHIPS * 2 * BINS, (phase + 1) * CHIPS * 2 * BINS)
        for j in range(2):
            sums = whole[:, j].reshape(CHIPS * 2 * BINS, C).astype(jnp.bfloat16)
            result[j] += lax.dot_general(sums, lags[rows], (((0,), (0,)), ((), ())),
                                         preferred_element_type=jnp.float32)
    for j in range(2):
        out_ref[j] = result[j].astype(jnp.bfloat16)

    def drain(t, _):
        @pl.when(jnp.logical_or(t != z, zh != core))
        def _():
            white_copy(PHASES - 1, t).wait_send()
        return 0

    lax.fori_loop(0, CHIPS, drain, 0)

    def drain_more(s, _):
        for phase in range(PHASES):
            rim_copy(phase, s).wait_send()
            for block in range(2):
                @pl.when(res_is_remote(block, s))
                def _():
                    res_copy(phase, block, s).wait_send()
        return 0

    lax.fori_loop(0, SEGS, drain_more, 0)
    for half in range(2):
        @pl.when(off_is_remote(half))
        def _():
            off_copy(half).wait_send()


def shards(columns, records, alive, offsets):
    vmem = pl.BlockSpec(memory_space=pltpu.VMEM)
    dma = pltpu.SemaphoreType.DMA
    call = pl.pallas_call(
        functools.partial(kernel, columns),
        out_shape=jax.ShapeDtypeStruct((2, C, NL), jnp.bfloat16),
        in_specs=[pl.BlockSpec(memory_space=pltpu.HBM)] * 4,
        out_specs=vmem,
        scratch_shapes=[
            pltpu.VMEM((1, C, W, WIN), jnp.bfloat16),
            pltpu.VMEM((1, C), jnp.int32),
            pltpu.VMEM((1, K), jnp.int32),
            pltpu.VMEM((2 * NF, WIN + NL), jnp.float32),
            pltpu.VMEM((W, PHASES * CHIPS, 2 * BINS, C), jnp.float32),
            pltpu.VMEM((PHASES, CHIPS, 2, ROWS, C), jnp.bfloat16),
            pltpu.VMEM((PHASES, 2, 2, SEGS, ROWS, C), jnp.bfloat16),
            pltpu.VMEM((PHASES, 2, SEGS, ROWS, C), jnp.bfloat16),
            pltpu.VMEM((2, 3 * C, LANES), jnp.float32),
            pltpu.VMEM((2, 2 * C, LANES), jnp.bfloat16),
            pltpu.VMEM((GROUP * C, 2 * LANES), jnp.bfloat16),
            pltpu.VMEM((PHASES, 2, SEGS, 4 * BINS, C), jnp.bfloat16),
            pltpu.VMEM((PHASES, CHIPS, 4 * BINS, C), jnp.bfloat16),
            pltpu.VMEM((8, LANES), jnp.int32),
            pltpu.VMEM((2, 8, LANES), jnp.int32),
            pltpu.SMEM((2, 8, LANES), jnp.int32),
            dma((PHASES, CHIPS)),
            dma((PHASES, 2, SEGS)),
            dma((PHASES, SEGS)),
            dma((PHASES, SEGS)),
            dma((PHASES, 2, SEGS)),
            dma((PHASES, CHIPS)),
            dma((2,)),
            dma((2,)),
            dma((2,)),
            dma((4,)),
        ],
        compiler_params=pltpu.CompilerParams(
            collective_id=0, has_side_effects=True, vmem_limit_bytes=53 * 1024 * 1024),
        cost_estimate=pl.CostEstimate(flops=400_000_000, bytes_accessed=3_000_000, transcendentals=1024),
        name="line_correlate",
    )
    return call(records, alive.reshape(1, C), offsets, tables())


def solution(mesh):
    in_specs = (P("seg", "chan", None, None), P("chan"), P("chan", None))
    out_specs = P("seg", "chan", None)
    body = functools.partial(shards, mesh.shape["chan"] // 4)
    return jax.shard_map(body, mesh=mesh, in_specs=in_specs, out_specs=out_specs, check_vma=False)
```
